768 devices in a mesh: rows: 96 (over z, y), rep: 8 (over x, core).
Axes of the slice: x: 4, y: 8, z: 12, core: 2. Of those that a mesh axis runs over, the one named last changes fastest.
Arguments:
- features: bfloat16 [98304, 256], P(('rows', 'rep')), may hold values from -6 to 6
- tile_table: bfloat16 [64, 64, 64], replicated, may hold values from -0.375 to 0.375
- weight: bfloat16 [256, 256], replicated, may hold values from -0.375 to 0.375
- bias_term: float32 [256], replicated, may hold values from -3 to 3
- cotangent: bfloat16 [98304, 256], P(('rows', 'rep')), may hold values from -6 to 6
- adj_rows: int32 [96, 8, 48], P('rows', 'rep'), may hold values from 0 to 15
- adj_cols: int32 [96, 8, 48], P('rows', 'rep'), may hold values from 0 to 191
- adj_tiles: int32 [96, 8, 48], P('rows', 'rep'), may hold values from 0 to 63
- adj_count: int32 [96, 8], P('rows', 'rep'), may hold values from 12 to 48, as said below
Outputs:
- output: bfloat16 [98304, 256], P(('rows', 'rep'))
- weight_grad: float32 [256, 256], replicated
- bias_grad: float32 [256], replicated
The draws below stay inside these ranges and needn't reach their ends.
Inputs may be any that keep to these rules, and one draw needn't show every extreme that they name: Slots at and beyond adj_count hold no entry; some list fills all 48 slots.
All inputs are finite; a program needn't handle non-finite values.
Results may differ from the reference program's by a relative error of at most 0.015.
Values may be sent and summed in bfloat16 or wider, within the bound.
No kernel may reach another device: no remote copies, remote signals or barrier semaphores. Data moves between devices by JAX's collectives and lax.ppermute only.
A program may use at most 32 MiB of HBM per device.

```python
import math
import jax
import jax.numpy as jnp
from jax import lax

BLOCK = 64
F = 256
BPD = 2
SLOTS = 48
TILES = 64
PANELS = 96
REPL = 8
NV = 98304


def draw_adj_cols(key, part):
    shape = (PANELS, REPL, SLOTS)
    near = jax.random.randint(jax.random.fold_in(key, 11), shape, 0, 2)
    offset = jax.random.randint(jax.random.fold_in(key, 12), shape, -2, 3)
    distant = jax.random.randint(jax.random.fold_in(key, 13), shape, 0, PANELS)
    within = jax.random.randint(jax.random.fold_in(key, 14), shape, 0, BPD)
    panel_ids = jnp.arange(PANELS, dtype=jnp.int32)[:, None, None]
    source = jnp.where(near == 1, (panel_ids + offset) % PANELS, distant)
    return (source * BPD + within).astype(jnp.int32)


def draw_adj_count(key, part):
    counts = jax.random.randint(jax.random.fold_in(key, 21), (PANELS * REPL,), SLOTS // 4, SLOTS + 1)
    fullest = jax.random.randint(jax.random.fold_in(key, 22), (), 0, PANELS * REPL)
    counts = jnp.where(jnp.arange(PANELS * REPL, dtype=jnp.int32) == fullest, SLOTS, counts)
    return counts.reshape(PANELS, REPL).astype(jnp.int32)


def place_ends(values, stream_key, smallest, largest):
    shape = values.shape
    index_at = [jax.random.randint(jax.random.fold_in(stream_key, axis), (), 0, shape[axis]) for axis in range(len(shape))]
    values = values.at[tuple(index_at)].set(smallest)
    longest = shape.index(max(shape))
    index_at[longest] = (index_at[longest] + 1) % shape[longest]
    return values.at[tuple(index_at)].set(largest)


def block_levels(key, dims, split, least, largest):
    loudness = 1.0
    for dim, shards_of in split:
        draws = jax.random.uniform(jax.random.fold_in(jax.random.fold_in(key, 6), dim), (shards_of,), jnp.float32, least / len(split), largest / len(split))
        loudness = loudness * jnp.repeat(jnp.exp(draws), dims[dim] // shards_of).reshape((-1,) + (1,) * (len(dims) - 1 - dim))
    return loudness


def centred(own_key, shape, spread, most, pieces=(), kind=jnp.bfloat16):
    entries = jax.random.normal(own_key, shape, jnp.float32) * spread
    if len(pieces) > 0:
        entries = block_levels(own_key, shape, pieces, -0.22, 0.18) * entries
    return jnp.clip(entries, min=-most, max=most).astype(kind)


def setup_inputs(seed: int = 0) -> dict:
    seeds = jax.random.split(jax.random.key(seed), 10)
    return {
        "features": centred(seeds[0], (NV, F), 1.0, 6.0, ((0, 768),)),
        "tile_table": centred(seeds[1], (TILES, BLOCK, BLOCK), (4 * BLOCK) ** -0.5, 0.375),
        "weight": centred(seeds[2], (F, F), F ** -0.5, 0.375),
        "bias_term": centred(seeds[3], (F,), 0.5, 3.0, (), jnp.float32),
        "cotangent": centred(seeds[4], (NV, F), 1.0, 6.0, ((0, 768),)),
        "adj_rows": place_ends(jax.random.randint(seeds[5], (PANELS, REPL, SLOTS), 0, REPL * BPD), jax.random.fold_in(seeds[5], 1), 0, (REPL * BPD) - 1).astype(jnp.int32),
        "adj_cols": draw_adj_cols(jax.random.fold_in(seeds[9], 71), 0),
        "adj_tiles": place_ends(jax.random.randint(seeds[7], (PANELS, REPL, SLOTS), 0, TILES), jax.random.fold_in(seeds[7], 1), 0, TILES - 1).astype(jnp.int32),
        "adj_count": draw_adj_count(jax.random.fold_in(seeds[9], 71), 0),
    }


def reference(features, tile_table, weight, bias_term, cotangent, adj_rows, adj_cols, adj_tiles, adj_count):
    blocks = features.reshape(NV // BLOCK, BLOCK, F)
    slot_ids = jnp.arange(SLOTS, dtype=jnp.int32)
    rep_ids = jnp.arange(REPL, dtype=jnp.int32)
    row_ids = jnp.arange(REPL * BPD, dtype=jnp.int32)

    def one_panel(carry, item):
        rows_in, cols_in, tile_ids, live_count = item
        cols_in = cols_in.astype(jnp.int32)
        column_block = (cols_in // BPD * REPL + rep_ids[:, None]) * BPD + cols_in % BPD
        picked = blocks[column_block.astype(jnp.int32)].astype(jnp.float32)
        chosen = tile_table[tile_ids.astype(jnp.int32)].astype(jnp.float32)
        products = jnp.einsum('csij,csjf->csif', chosen, picked)
        live = slot_ids[None, :] < live_count[:, None].astype(jnp.int32)
        onehot = ((rows_in.astype(jnp.int32)[:, :, None] == row_ids[None, None, :]) & live[:, :, None]).astype(jnp.float32)
        summed = jnp.einsum('csr,csif->rif', onehot, products)
        return (carry, summed)
    _, panels = lax.scan(one_panel, jnp.zeros((), jnp.float32), (adj_rows, adj_cols, adj_tiles, adj_count))
    agg = panels.reshape(NV, F).astype(jnp.bfloat16)
    pre = jnp.dot(agg, weight, preferred_element_type=jnp.float32) + bias_term
    output = jax.nn.silu(pre).astype(jnp.bfloat16)
    sigma = jax.nn.sigmoid(pre)
    grad_pre = (cotangent.astype(jnp.float32) * (sigma * (1.0 + pre * (1.0 - sigma)))).astype(jnp.bfloat16)
    factor = 1.0 / math.sqrt(NV)
    weight_grad = lax.dot_general(agg, grad_pre, (((0,), (0,)), ((), ())), preferred_element_type=jnp.float32) * factor
    bias_grad = lax.optimization_barrier(jnp.sum(grad_pre.astype(jnp.float32), axis=0)) * factor
    return (output, weight_grad, bias_grad)
```

```python
import functools
import math

import jax
import jax.numpy as jnp
from jax import lax
from jax.experimental import pallas as pl
from jax.experimental.pallas import tpu as pltpu
from jax.sharding import PartitionSpec as P

BLOCK = 64
BPD = 2
UNROLL = 4


def spmm_kernel(
    rows_ref,
    cols_ref,
    tiles_ref,
    count_ref,
    features_ref,
    table_ref,
    out_ref,
    picked,
    table,
    total,
    sems,
    table_sem,
):
    count = count_ref[0, 0]

    def fetch(s):
        start = pl.multiple_of(cols_ref[0, 0, s] * BLOCK, BLOCK)
        return pltpu.make_async_copy(
            features_ref.at[pl.ds(start, BLOCK)], picked.at[s], sems.at[s]
        )

    steps = (count + UNROLL - 1) // UNROLL
    table_copy = pltpu.make_async_copy(table_ref, table, table_sem)
    table_copy.start()

    def begin(i, carry):
        for k in range(UNROLL):
            fetch(i * UNROLL + k).start()
        return carry

    lax.fori_loop(0, steps, begin, 0)
    total[...] = jnp.zeros_like(total)
    table_copy.wait()

    def step(i, carry):
        products = []
        for k in range(UNROLL):
            s = i * UNROLL + k
            fetch(s).wait()
            product = jnp.dot(
                table[tiles_ref[0, 0, s]], picked[s], preferred_element_type=jnp.float32
            )
            products.append(jnp.where(s < count, product, 0.0))
        for k in range(UNROLL):
            row = pl.multiple_of(rows_ref[0, 0, i * UNROLL + k] * BLOCK, BLOCK)
            total[pl.ds(row, BLOCK)] += products[k]
        return carry

    lax.fori_loop(0, steps, step, 0)
    out_ref[...] = total[...].astype(out_ref.dtype)


def spmm(adj_rows, adj_cols, adj_tiles, adj_count, gathered, tile_table, out_rows):
    slots = adj_rows.shape[-1]
    width = gathered.shape[1]
    smem = pl.BlockSpec(memory_space=pltpu.SMEM)
    hbm = pl.BlockSpec(memory_space=pltpu.HBM)
    return pl.pallas_call(
        spmm_kernel,
        out_shape=jax.ShapeDtypeStruct((out_rows, width), jnp.bfloat16),
        in_specs=[smem, smem, smem, smem, hbm, hbm],
        out_specs=pl.BlockSpec(memory_space=pltpu.VMEM),
        scratch_shapes=[
            pltpu.VMEM((slots, BLOCK, width), jnp.bfloat16),
            pltpu.VMEM(tile_table.shape, tile_table.dtype),
            pltpu.VMEM((out_rows, width), jnp.float32),
            pltpu.SemaphoreType.DMA((slots,)),
            pltpu.SemaphoreType.DMA,
        ],
        compiler_params=pltpu.CompilerParams(vmem_limit_bytes=58 * 1024 * 1024),
        name="spmm",
    )(adj_rows, adj_cols, adj_tiles, adj_count, gathered, tile_table)


def layer_kernel(factor, parts_ref, weight_ref, bias_ref, cotangent_ref, out_ref, grads_ref):
    summed = parts_ref[0].astype(jnp.float32)
    for r in range(1, parts_ref.shape[0]):
        summed += parts_ref[r].astype(jnp.float32)
    agg = summed.astype(jnp.bfloat16)
    pre = jnp.dot(agg, weight_ref[...], preferred_element_type=jnp.float32) + bias_ref[...]
    sigma = 1.0 / (1.0 + jnp.exp(-pre))
    out_ref[...] = (pre * sigma).astype(out_ref.dtype)
    grad_pre = (
        cotangent_ref[...].astype(jnp.float32) * (sigma * (1.0 + pre * (1.0 - sigma)))
    ).astype(jnp.bfloat16)
    width = grad_pre.shape[1]
    grads_ref[:width] = factor * lax.dot_general(
        agg, grad_pre, (((0,), (0,)), ((), ())), preferred_element_type=jnp.float32
    )
    bias = factor * jnp.sum(grad_pre.astype(jnp.float32), axis=0, keepdims=True)
    first = lax.broadcasted_iota(jnp.int32, (8, width), 0) == 0
    grads_ref[width:] = jnp.where(first, bias, 0.0)


def layer(parts, weight, bias_term, cotangent, factor):
    width = weight.shape[0]
    vmem = pl.BlockSpec(memory_space=pltpu.VMEM)
    return pl.pallas_call(
        functools.partial(layer_kernel, factor),
        out_shape=(
            jax.ShapeDtypeStruct(cotangent.shape, jnp.bfloat16),
            jax.ShapeDtypeStruct((width + 8, width), jnp.float32),
        ),
        in_specs=[vmem] * 4,
        out_specs=(vmem, vmem),
        compiler_params=pltpu.CompilerParams(vmem_limit_bytes=16 * 1024 * 1024),
        name="layer",
    )(parts, weight, bias_term.reshape(1, -1), cotangent)


def shards(
    features, tile_table, weight, bias_term, cotangent, adj_rows, adj_cols, adj_tiles, adj_count
):
    own_rows, width = features.shape
    rep_size = lax.axis_size("rep")
    gathered = lax.all_gather(features, "rows", axis=0, tiled=True)
    share = spmm(
        adj_rows, adj_cols, adj_tiles, adj_count, gathered, tile_table, rep_size * own_rows
    )
    parts = lax.all_to_all(
        share.reshape(rep_size, own_rows, width), "rep", split_axis=0, concat_axis=0, tiled=True
    )
    factor = 1.0 / math.sqrt(lax.axis_size("rows") * rep_size * own_rows)
    output, grads = layer(parts, weight, bias_term, cotangent, factor)
    grads = lax.psum(grads, ("rows", "rep"))
    return (output, grads[:width], grads[width])


def solution(mesh):
    return jax.shard_map(
        shards,
        mesh=mesh,
        in_specs=(
            P(("rows", "rep"), None),
            P(),
            P(),
            P(),
            P(("rows", "rep"), None),
            P("rows", "rep", None),
            P("rows", "rep", None),
            P("rows", "rep", None),
            P("rows", "rep"),
        ),
        out_specs=(P(("rows", "rep"), None), P(), P()),
        check_vma=False,
    )
```

```python
import functools
import math

import jax
import jax.numpy as jnp
import numpy as np
from jax import lax
from jax.experimental import pallas as pl
from jax.experimental.pallas import tpu as pltpu
from jax.sharding import Mesh, PartitionSpec as P

BLOCK = 64
BPD = 2
UNROLL = 4
HALF = 128
MIB = 1024 * 1024
REP = ("x", "core")
SMEM = pl.BlockSpec(memory_space=pltpu.SMEM)
HBM = pl.BlockSpec(memory_space=pltpu.HBM)
VMEM = pl.BlockSpec(memory_space=pltpu.VMEM)


def spmm_kernel(
    place,
    rows_ref,
    cols_ref,
    tiles_ref,
    count_ref,
    features_ref,
    table_ref,
    out_ref,
    picked,
    table,
    total,
    sems,
    table_sem,
):
    count = count_ref[0, 0]

    def fetch(s):
        start = pl.multiple_of(place(cols_ref[0, 0, s]) * BLOCK, BLOCK)
        return pltpu.make_async_copy(
            features_ref.at[pl.ds(start, BLOCK)], picked.at[s], sems.at[s]
        )

    steps = (count + UNROLL - 1) // UNROLL
    table_copy = pltpu.make_async_copy(table_ref, table, table_sem)
    table_copy.start()

    def begin(i, carry):
        for k in range(UNROLL):
            fetch(i * UNROLL + k).start()
        return carry

    lax.fori_loop(0, steps, begin, 0)
    total[...] = jnp.zeros_like(total)
    table_copy.wait()

    def step(i, carry):
        products = []
        for k in range(UNROLL):
            s = i * UNROLL + k
            fetch(s).wait()
            product = jnp.dot(
                table[tiles_ref[0, 0, s]], picked[s], preferred_element_type=jnp.float32
            )
            products.append(jnp.where(s < count, product, 0.0))
        for k in range(UNROLL):
            row = pl.multiple_of(rows_ref[0, 0, i * UNROLL + k] * BLOCK, BLOCK)
            total[pl.ds(row, BLOCK)] += products[k]
        return carry

    lax.fori_loop(0, steps, step, 0)
    out_ref[...] = total[...].astype(out_ref.dtype)


def spmm(place, lists, gathered, tile_table, out_rows):
    slots = lists[0].shape[-1]
    width = gathered.shape[1]
    return pl.pallas_call(
        functools.partial(spmm_kernel, place),
        out_shape=jax.ShapeDtypeStruct((out_rows, width), jnp.bfloat16),
        in_specs=[SMEM, SMEM, SMEM, SMEM, HBM, HBM],
        out_specs=VMEM,
        scratch_shapes=[
            pltpu.VMEM((slots, BLOCK, width), jnp.bfloat16),
            pltpu.VMEM(tile_table.shape, tile_table.dtype),
            pltpu.VMEM((out_rows, width), jnp.float32),
            pltpu.SemaphoreType.DMA((slots,)),
            pltpu.SemaphoreType.DMA,
        ],
        compiler_params=pltpu.CompilerParams(vmem_limit_bytes=58 * MIB),
        name="spmm",
    )(*lists, gathered, tile_table)


def layer_kernel(
    factor, left_ref, right_ref, weight_ref, bias_ref, cotangent_ref, out_ref, grads_ref
):
    def reduced(ref):
        summed = ref[0].astype(jnp.float32)
        for r in range(1, ref.shape[0]):
            summed += ref[r].astype(jnp.float32)
        return summed.astype(jnp.bfloat16)

    agg = jnp.concatenate([reduced(left_ref), reduced(right_ref)], axis=1)
    pre = jnp.dot(agg, weight_ref[...], preferred_element_type=jnp.float32) + bias_ref[...]
    sigma = 1.0 / (1.0 + jnp.exp(-pre))
    out_ref[...] = (pre * sigma).astype(out_ref.dtype)
    grad_pre = (
        cotangent_ref[...].astype(jnp.float32) * (sigma * (1.0 + pre * (1.0 - sigma)))
    ).astype(jnp.bfloat16)
    width = grad_pre.shape[1]
    grads_ref[:width] = factor * lax.dot_general(
        agg, grad_pre, (((0,), (0,)), ((), ())), preferred_element_type=jnp.float32
    )
    bias = factor * jnp.sum(grad_pre.astype(jnp.float32), axis=0, keepdims=True)
    extra = grads_ref.shape[0] - width
    first = lax.broadcasted_iota(jnp.int32, (extra, width), 0) == 0
    grads_ref[width:] = jnp.where(first, bias, 0.0)


def layer(left, right, weight, bias_term, cotangent, factor):
    width = weight.shape[0]
    return pl.pallas_call(
        functools.partial(layer_kernel, factor),
        out_shape=(
            jax.ShapeDtypeStruct(cotangent.shape, jnp.bfloat16),
            jax.ShapeDtypeStruct((width + 64, width), jnp.float32),
        ),
        in_specs=[VMEM] * 5,
        out_specs=(VMEM, VMEM),
        compiler_params=pltpu.CompilerParams(vmem_limit_bytes=16 * MIB),
        name="layer",
    )(left, right, weight, bias_term.reshape(1, -1), cotangent)


def spread(array, axis):
    copies = jnp.broadcast_to(array[None], (lax.axis_size(axis),) + array.shape)
    return lax.all_to_all(copies, axis, split_axis=0, concat_axis=0, tiled=True)


def scattered(array, axis):
    size = lax.axis_size(axis)
    parts = array.reshape(size, array.shape[0] // size, array.shape[1])
    return lax.all_to_all(parts, axis, split_axis=0, concat_axis=0, tiled=True)


def total_over_all(grads):
    share = jnp.sum(scattered(grads, REP), axis=0)
    share = jnp.sum(spread(share, "y"), axis=0)
    share = jnp.sum(spread(share, "z"), axis=0)
    return lax.all_gather(share, REP, axis=0, tiled=True)


def shards(
    features, tile_table, weight, bias_term, cotangent, adj_rows, adj_cols, adj_tiles, adj_count
):
    own_rows, width = features.shape
    rep_size = lax.axis_size(REP)
    lists = (adj_rows, adj_cols, adj_tiles, adj_count)
    ny, nz = lax.axis_size("y"), lax.axis_size("z")
    near_y = spread(features[:, :HALF], "y").reshape(ny * own_rows, HALF)
    near_z = spread(features[:, HALF:], "z").reshape(nz * own_rows, width - HALF)
    left = lax.all_gather(near_y, "z", axis=0, tiled=True)
    right = lax.all_gather(near_z, "y", axis=0, tiled=True)

    def by_z(col):
        return col

    def by_y(col):
        panel = col // BPD
        return ((panel % ny) * nz + panel // ny) * BPD + col % BPD

    rows = rep_size * own_rows
    left = scattered(spmm(by_z, lists, left, tile_table, rows), REP)
    right = scattered(spmm(by_y, lists, right, tile_table, rows), REP)
    factor = 1.0 / math.sqrt(nz * ny * rows)
    output, grads = layer(left, right, weight, bias_term, cotangent, factor)
    grads = total_over_all(grads)
    return (output, grads[:width], grads[width])


def solution(mesh):
    panels, rep = mesh.devices.shape
    ny = 8 if panels % 8 == 0 else 2
    devices = np.asarray(mesh.devices).reshape(panels // ny, ny, rep // 2, 2)
    rows = ("z", "y")
    return jax.shard_map(
        shards,
        mesh=Mesh(devices, ("z", "y", "x", "core")),
        in_specs=(
            P(rows + REP, None),
            P(),
            P(),
            P(),
            P(rows + REP, None),
            P(rows, REP, None),
            P(rows, REP, None),
            P(rows, REP, None),
            P(rows, REP),
        ),
        out_specs=(P(rows + REP, None), P(), P()),
        check_vma=False,
    )
```

```python
import functools
import math

import jax
import jax.numpy as jnp
import numpy as np
from jax import lax
from jax.experimental import pallas as pl
from jax.experimental.pallas import tpu as pltpu
from jax.sharding import Mesh, PartitionSpec as P

BLOCK = 64
BPD = 2
UNROLL = 12
HALF = 128
MIB = 1024 * 1024
REP = ("x", "core")
SMEM = pl.BlockSpec(memory_space=pltpu.SMEM)
HBM = pl.BlockSpec(memory_space=pltpu.HBM)
VMEM = pl.BlockSpec(memory_space=pltpu.VMEM)


def spmm_kernel(
    rows_ref, tiles_ref, count_ref, which_ref, start_ref, table_ref, *refs
):
    *sources, out_ref, picked, table, total, sems, table_sem = refs
    count = count_ref[0, 0]

    def fetch(s, source, start):
        return pltpu.make_async_copy(
            source.at[pl.ds(start, BLOCK)], picked.at[s], sems.at[s]
        )

    steps = (count + UNROLL - 1) // UNROLL
    table_copy = pltpu.make_async_copy(table_ref, table, table_sem)
    table_copy.start()

    def begin(i, carry):
        for k in range(UNROLL):
            s = i * UNROLL + k
            start = pl.multiple_of(start_ref[s], BLOCK)
            if len(sources) == 1:
                fetch(s, sources[0], start).start()
                continue
            for n, source in enumerate(sources):

                @pl.when(which_ref[s] == n)
                def _():
                    fetch(s, source, start).start()

        return carry

    lax.fori_loop(0, steps, begin, 0)
    total[...] = jnp.zeros_like(total)
    table_copy.wait()

    def step(i, carry):
        for k in range(UNROLL):
            fetch(i * UNROLL + k, sources[0], 0).wait()
        for k in range(UNROLL):
            s = i * UNROLL + k
            product = jnp.dot(
                table[tiles_ref[0, 0, s]], picked[s], preferred_element_type=jnp.float32
            )
            row = pl.multiple_of(rows_ref[0, 0, s] * BLOCK, BLOCK)
            total[pl.ds(row, BLOCK)] += jnp.where(s < count, product, 0.0)
        return carry

    lax.fori_loop(0, steps, step, 0)
    out_ref[...] = total[...].astype(out_ref.dtype)


def spmm(lists, which, start, sources, tile_table, out_rows):
    slots = start.shape[0]
    width = sources[0].shape[1]
    return pl.pallas_call(
        spmm_kernel,
        out_shape=jax.ShapeDtypeStruct((out_rows, width), jnp.bfloat16),
        in_specs=[SMEM] * 5 + [HBM] * (1 + len(sources)),
        out_specs=VMEM,
        scratch_shapes=[
            pltpu.VMEM((slots, BLOCK, width), jnp.bfloat16),
            pltpu.VMEM(tile_table.shape, tile_table.dtype),
            pltpu.VMEM((out_rows, width), jnp.float32),
            pltpu.SemaphoreType.DMA((slots,)),
            pltpu.SemaphoreType.DMA,
        ],
        compiler_params=pltpu.CompilerParams(vmem_limit_bytes=58 * MIB),
        name="spmm",
    )(*lists, which, start, tile_table, *sources)


def layer_kernel(
    factor, left_ref, right_ref, weight_ref, bias_ref, cotangent_ref, out_ref, grads_ref
):
    def reduced(ref):
        summed = ref[0].astype(jnp.float32)
        for r in range(1, ref.shape[0]):
            summed += ref[r].astype(jnp.float32)
        return summed.astype(jnp.bfloat16)

    agg = jnp.concatenate([reduced(left_ref), reduced(right_ref)], axis=1)
    pre = jnp.dot(agg, weight_ref[...], preferred_element_type=jnp.float32) + bias_ref[...]
    sigma = 1.0 / (1.0 + jnp.exp(-pre))
    out_ref[...] = (pre * sigma).astype(out_ref.dtype)
    grad_pre = (
        cotangent_ref[...].astype(jnp.float32) * (sigma * (1.0 + pre * (1.0 - sigma)))
    ).astype(jnp.bfloat16)
    width = grad_pre.shape[1]
    weight_grad = factor * lax.dot_general(
        agg, grad_pre, (((0,), (0,)), ((), ())), preferred_element_type=jnp.float32
    )
    grads_ref[:width] = weight_grad.astype(grads_ref.dtype)
    bias = factor * jnp.sum(grad_pre.astype(jnp.float32), axis=0, keepdims=True)
    extra = grads_ref.shape[0] - width
    first = lax.broadcasted_iota(jnp.int32, (extra, width), 0) == 0
    grads_ref[width:] = jnp.where(first, bias, 0.0).astype(grads_ref.dtype)


def layer(left, right, weight, bias_term, cotangent, factor, grad_rows):
    width = weight.shape[0]
    return pl.pallas_call(
        functools.partial(layer_kernel, factor),
        out_shape=(
            jax.ShapeDtypeStruct(cotangent.shape, jnp.bfloat16),
            jax.ShapeDtypeStruct((grad_rows, width), jnp.bfloat16),
        ),
        in_specs=[VMEM] * 5,
        out_specs=(VMEM, VMEM),
        compiler_params=pltpu.CompilerParams(vmem_limit_bytes=16 * MIB),
        name="layer",
    )(left, right, weight, bias_term.reshape(1, -1), cotangent)


def spread(array, axis):
    copies = jnp.broadcast_to(array[None], (lax.axis_size(axis),) + array.shape)
    return lax.all_to_all(copies, axis, split_axis=0, concat_axis=0, tiled=True)


def scattered(array, axis):
    size = lax.axis_size(axis)
    parts = array.reshape(size, array.shape[0] // size, array.shape[1])
    return lax.all_to_all(parts, axis, split_axis=0, concat_axis=0, tiled=True)


def summed(parts):
    total = parts[0].astype(jnp.float32)
    for part in parts[1:]:
        total += part.astype(jnp.float32)
    return total.astype(jnp.bfloat16)


def total_over_all(grads):
    share = summed(scattered(grads, "z"))
    share = summed(spread(share, "y"))
    share = summed(spread(share, REP))
    return spread(share, "z").reshape(grads.shape).astype(jnp.float32)


def both_ways(block, axis):
    n = lax.axis_size(axis)
    up = [(i, (i + 1) % n) for i in range(n)]
    down = [(i, (i - 1) % n) for i in range(n)]
    before, after = [block], [block]
    for _ in range(n // 2 - 1):
        before.append(lax.ppermute(before[-1], axis, up))
        after.append(lax.ppermute(after[-1], axis, down))
    half = block.shape[0] // 2
    far = [
        lax.ppermute(before[-1][:half], axis, up),
        lax.ppermute(after[-1][half:], axis, down),
    ]
    return before + after[:0:-1] + far


def shards(
    features, tile_table, weight, bias_term, cotangent, adj_rows, adj_cols, adj_tiles, adj_count
):
    own_rows, width = features.shape
    rep_size = lax.axis_size(REP)
    lists = (adj_rows, adj_tiles, adj_count)
    ny, nz = lax.axis_size("y"), lax.axis_size("z")
    near_y = spread(features[:, :HALF], "y").reshape(ny * own_rows, HALF)
    near_z = spread(features[:, HALF:], "z").reshape(nz * own_rows, width - HALF)
    left = lax.all_gather(near_y, "z", axis=0, tiled=True)
    right = both_ways(near_z, "y")

    cols = adj_cols[0, 0]
    panel = cols // BPD
    behind = (lax.axis_index("y") - panel) % ny
    start = (panel // ny * BPD + cols % BPD) * BLOCK
    half = near_z.shape[0] // 2
    upper = start >= half
    far = behind == ny // 2
    which = jnp.where(far, ny - 1 + upper.astype(jnp.int32), behind - (behind > ny // 2))
    start = jnp.where(far & upper, start - half, start)

    rows = rep_size * own_rows
    left = scattered(spmm(lists, which, cols * BLOCK, [left], tile_table, rows), REP)
    right = scattered(spmm(lists, which, start, right, tile_table, rows), REP)
    factor = 1.0 / math.sqrt(nz * ny * rows)
    grad_rows = -(-(width + 8) // (8 * nz)) * 8 * nz
    output, grads = layer(left, right, weight, bias_term, cotangent, factor, grad_rows)
    grads = total_over_all(grads)
    return (output, grads[:width], grads[width])


def solution(mesh):
    panels, rep = mesh.devices.shape
    ny = 8 if panels % 8 == 0 else 2
    devices = np.asarray(mesh.devices).reshape(panels // ny, ny, rep // 2, 2)
    rows = ("z", "y")
    return jax.shard_map(
        shards,
        mesh=Mesh(devices, ("z", "y", "x", "core")),
        in_specs=(
            P(rows + REP, None),
            P(),
            P(),
            P(),
            P(rows + REP, None),
            P(rows, REP, None),
            P(rows, REP, None),
            P(rows, REP, None),
            P(rows, REP),
        ),
        out_specs=(P(rows + REP, None), P(), P()),
        check_vma=False,
    )
```

```python
import functools
import math

import jax
import jax.numpy as jnp
import numpy as np
from jax import lax
from jax.experimental import pallas as pl
from jax.experimental.pallas import tpu as pltpu
from jax.sharding import Mesh, PartitionSpec as P

BLOCK = 64
BPD = 2
UNROLL = 12
LEAD = 16
ALIGN = 16
MIB = 1024 * 1024
REP = ("x", "core")
SMEM = pl.BlockSpec(memory_space=pltpu.SMEM)
HBM = pl.BlockSpec(memory_space=pltpu.HBM)
VMEM = pl.BlockSpec(memory_space=pltpu.VMEM)


def spmm_kernel(
    rows_ref, tiles_ref, count_ref, near_ref, which_ref, start_ref, table_ref, *refs
):
    near, *ring, out_ref, picked, table, total, sems, table_sem = refs
    count = count_ref[0, 0]
    steps = (count + UNROLL - 1) // UNROLL
    table_copy = pltpu.make_async_copy(table_ref, table, table_sem)
    table_copy.start()

    def fetch(s, source, start, rows, at):
        return pltpu.make_async_copy(
            source.at[pl.ds(pl.multiple_of(start, ALIGN), rows)],
            picked.at[s, pl.ds(at, rows)],
            sems.at[s],
        )

    def begin(i, carry):
        for k in range(UNROLL):
            s = i * UNROLL + k

            @pl.when(which_ref[s] < 0)
            def _():
                fetch(s, near, near_ref[s], BLOCK, 0).start()

            @pl.when(which_ref[s] >= 0)
            def _():
                fetch(s, near, near_ref[s], LEAD, 0).start()
                for n, source in enumerate(ring):

                    @pl.when(which_ref[s] == n)
                    def _():
                        fetch(s, source, start_ref[s], BLOCK - LEAD, LEAD).start()

        return carry

    lax.fori_loop(0, steps, begin, 0)
    total[...] = jnp.zeros_like(total)
    table_copy.wait()

    def step(i, carry):
        for k in range(UNROLL):
            fetch(i * UNROLL + k, near, 0, BLOCK, 0).wait()
        for k in range(UNROLL):
            s = i * UNROLL + k
            product = jnp.dot(
                table[tiles_ref[0, 0, s]], picked[s], preferred_element_type=jnp.float32
            )
            row = pl.multiple_of(rows_ref[0, 0, s] * BLOCK, BLOCK)
            total[pl.ds(row, BLOCK)] += jnp.where(s < count, product, 0.0)
        return carry

    lax.fori_loop(0, steps, step, 0)
    out_ref[...] = total[...].astype(out_ref.dtype)


def spmm(lists, near_start, which, start, near, ring, tile_table, out_rows):
    slots = start.shape[0]
    width = near.shape[1]
    return pl.pallas_call(
        spmm_kernel,
        out_shape=jax.ShapeDtypeStruct((out_rows, width), jnp.bfloat16),
        in_specs=[SMEM] * 6 + [HBM] * (2 + len(ring)),
        out_specs=VMEM,
        scratch_shapes=[
            pltpu.VMEM((slots, BLOCK, width), jnp.bfloat16),
            pltpu.VMEM(tile_table.shape, tile_table.dtype),
            pltpu.VMEM((out_rows, width), jnp.float32),
            pltpu.SemaphoreType.DMA((slots,)),
            pltpu.SemaphoreType.DMA,
        ],
        compiler_params=pltpu.CompilerParams(vmem_limit_bytes=58 * MIB),
        name="spmm",
    )(*lists, near_start, which, start, tile_table, near, *ring)


def layer_kernel(
    factor, parts_ref, weight_ref, bias_ref, cotangent_ref, out_ref, grads_ref
):
    summed = parts_ref[0].astype(jnp.float32)
    for r in range(1, parts_ref.shape[0]):
        summed += parts_ref[r].astype(jnp.float32)
    agg = summed.astype(jnp.bfloat16)
    pre = jnp.dot(agg, weight_ref[...], preferred_element_type=jnp.float32) + bias_ref[...]
    sigma = 1.0 / (1.0 + jnp.exp(-pre))
    out_ref[...] = (pre * sigma).astype(out_ref.dtype)
    grad_pre = (
        cotangent_ref[...].astype(jnp.float32) * (sigma * (1.0 + pre * (1.0 - sigma)))
    ).astype(jnp.bfloat16)
    width = grad_pre.shape[1]
    weight_grad = factor * lax.dot_general(
        agg, grad_pre, (((0,), (0,)), ((), ())), preferred_element_type=jnp.float32
    )
    grads_ref[:width] = weight_grad.astype(grads_ref.dtype)
    bias = factor * jnp.sum(grad_pre.astype(jnp.float32), axis=0, keepdims=True)
    extra = grads_ref.shape[0] - width
    first = lax.broadcasted_iota(jnp.int32, (extra, width), 0) == 0
    grads_ref[width:] = jnp.where(first, bias, 0.0).astype(grads_ref.dtype)


def layer(parts, weight, bias_term, cotangent, factor, grad_rows):
    width = weight.shape[0]
    return pl.pallas_call(
        functools.partial(layer_kernel, factor),
        out_shape=(
            jax.ShapeDtypeStruct(cotangent.shape, jnp.bfloat16),
            jax.ShapeDtypeStruct((grad_rows, width), jnp.bfloat16),
        ),
        in_specs=[VMEM] * 4,
        out_specs=(VMEM, VMEM),
        compiler_params=pltpu.CompilerParams(vmem_limit_bytes=16 * MIB),
        name="layer",
    )(parts, weight, bias_term.reshape(1, -1), cotangent)


def spread(array, axis):
    copies = jnp.broadcast_to(array[None], (lax.axis_size(axis),) + array.shape)
    return lax.all_to_all(copies, axis, split_axis=0, concat_axis=0, tiled=True)


def scattered(array, axis):
    size = lax.axis_size(axis)
    parts = array.reshape(size, array.shape[0] // size, array.shape[1])
    return lax.all_to_all(parts, axis, split_axis=0, concat_axis=0, tiled=True)


def summed(parts):
    total = parts[0].astype(jnp.float32)
    for part in parts[1:]:
        total += part.astype(jnp.float32)
    return total.astype(jnp.bfloat16)


def total_over_all(grads):
    share = summed(scattered(grads, "z"))
    share = summed(spread(share, "y"))
    share = summed(spread(share, REP))
    return spread(share, "z").reshape(grads.shape).astype(jnp.float32)


def both_ways(block, axis):
    n = lax.axis_size(axis)
    up = [(i, (i + 1) % n) for i in range(n)]
    down = [(i, (i - 1) % n) for i in range(n)]
    before, after = [block], [block]
    for _ in range(n // 2 - 1):
        before.append(lax.ppermute(before[-1], axis, up))
        after.append(lax.ppermute(after[-1], axis, down))
    half = block.shape[0] // 2
    far = [
        lax.ppermute(before[-1][:half], axis, up),
        lax.ppermute(after[-1][half:], axis, down),
    ]
    return before + after[:0:-1] + far


def shards(
    features, tile_table, weight, bias_term, cotangent, adj_rows, adj_cols, adj_tiles, adj_count
):
    own_rows, width = features.shape
    rep_size = lax.axis_size(REP)
    lists = (adj_rows, adj_tiles, adj_count)
    ny, nz = lax.axis_size("y"), lax.axis_size("z")
    kept = BLOCK + LEAD
    near = spread(features[:kept], "y").reshape(ny * kept, width)
    near = lax.all_gather(near, "z", axis=0, tiled=True)
    ring = both_ways(lax.all_gather(features[kept:], "z", axis=0, tiled=True), "y")

    cols = adj_cols[0, 0]
    panel = cols // BPD
    second = cols % BPD == 1
    near_start = panel * kept + jnp.where(second, BLOCK, 0)
    behind = (lax.axis_index("y") - panel) % ny
    start = panel // ny * (own_rows - kept)
    half = ring[-1].shape[0]
    upper = start >= half
    far = behind == ny // 2
    which = jnp.where(far, ny - 1 + upper.astype(jnp.int32), behind - (behind > ny // 2))
    which = jnp.where(second, which, -1)
    start = jnp.where(far & upper, start - half, start)

    rows = rep_size * own_rows
    share = spmm(lists, near_start, which, start, near, ring, tile_table, rows)
    parts = scattered(share, REP)
    factor = 1.0 / math.sqrt(nz * ny * rows)
    grad_rows = -(-(width + 8) // (8 * nz)) * 8 * nz
    output, grads = layer(parts, weight, bias_term, cotangent, factor, grad_rows)
    grads = total_over_all(grads)
    return (output, grads[:width], grads[width])


def solution(mesh):
    panels, rep = mesh.devices.shape
    ny = 8 if panels % 8 == 0 else 2
    devices = np.asarray(mesh.devices).reshape(panels // ny, ny, rep // 2, 2)
    rows = ("z", "y")
    return jax.shard_map(
        shards,
        mesh=Mesh(devices, ("z", "y", "x", "core")),
        in_specs=(
            P(rows + REP, None),
            P(),
            P(),
            P(),
            P(rows + REP, None),
            P(rows, REP, None),
            P(rows, REP, None),
            P(rows, REP, None),
            P(rows, REP),
        ),
        out_specs=(P(rows + REP, None), P(), P()),
        check_vma=False,
    )
```

```python
import functools
import math

import jax
import jax.numpy as jnp
import numpy as np
from jax import lax
from jax.experimental import pallas as pl
from jax.experimental.pallas import tpu as pltpu
from jax.sharding import Mesh, PartitionSpec as P

BLOCK = 64
BPD = 2
UNROLL = 12
LEAD = 16
ALIGN = 16
MIB = 1024 * 1024
REP = ("x", "core")
SMEM = pl.BlockSpec(memory_space=pltpu.SMEM)
HBM = pl.BlockSpec(memory_space=pltpu.HBM)
VMEM = pl.BlockSpec(memory_space=pltpu.VMEM)


def spmm_kernel(
    rows_ref, tiles_ref, count_ref, near_ref, which_ref, start_ref, table_ref, *refs
):
    near, *ring, out_ref, picked, table, total, sems, table_sem = refs
    count = count_ref[0, 0]
    steps = (count + UNROLL - 1) // UNROLL
    table_copy = pltpu.make_async_copy(table_ref, table, table_sem)
    table_copy.start()

    def fetch(s, source, start, rows, at):
        return pltpu.make_async_copy(
            source.at[pl.ds(pl.multiple_of(start, ALIGN), rows)],
            picked.at[s, pl.ds(at, rows)],
            sems.at[s],
        )

    def begin(i, carry):
        for k in range(UNROLL):
            s = i * UNROLL + k

            @pl.when(which_ref[s] < 0)
            def _():
                fetch(s, near, near_ref[s], BLOCK, 0).start()

            @pl.when(which_ref[s] >= 0)
            def _():
                fetch(s, near, near_ref[s], LEAD, 0).start()
                for n, source in enumerate(ring):

                    @pl.when(which_ref[s] == n)
                    def _():
                        fetch(s, source, start_ref[s], BLOCK - LEAD, LEAD).start()

        return carry

    lax.fori_loop(0, steps, begin, 0)
    total[...] = jnp.zeros_like(total)
    table_copy.wait()

    def step(i, carry):
        for k in range(UNROLL):
            fetch(i * UNROLL + k, near, 0, BLOCK, 0).wait()
        for k in range(UNROLL):
            s = i * UNROLL + k
            product = jnp.dot(
                table[tiles_ref[0, 0, s]], picked[s], preferred_element_type=jnp.float32
            )
            row = pl.multiple_of(rows_ref[0, 0, s] * BLOCK, BLOCK)
            total[pl.ds(row, BLOCK)] += jnp.where(s < count, product, 0.0)
        return carry

    lax.fori_loop(0, steps, step, 0)
    out_ref[...] = total[...].astype(out_ref.dtype)


def spmm(lists, near_start, which, start, near, ring, tile_table, out_rows):
    slots = start.shape[0]
    width = near.shape[1]
    return pl.pallas_call(
        spmm_kernel,
        out_shape=jax.ShapeDtypeStruct((out_rows, width), jnp.bfloat16),
        in_specs=[SMEM] * 6 + [HBM] * (2 + len(ring)),
        out_specs=VMEM,
        scratch_shapes=[
            pltpu.VMEM((slots, BLOCK, width), jnp.bfloat16),
            pltpu.VMEM(tile_table.shape, tile_table.dtype),
            pltpu.VMEM((out_rows, width), jnp.float32),
            pltpu.SemaphoreType.DMA((slots,)),
            pltpu.SemaphoreType.DMA,
        ],
        compiler_params=pltpu.CompilerParams(vmem_limit_bytes=58 * MIB),
        name="spmm",
    )(*lists, near_start, which, start, tile_table, near, *ring)


def layer_kernel(
    factor, parts_ref, weight_ref, bias_ref, cotangent_ref, out_ref, grads_ref
):
    summed = parts_ref[0].astype(jnp.float32)
    for r in range(1, parts_ref.shape[0]):
        summed += parts_ref[r].astype(jnp.float32)
    agg = summed.astype(jnp.bfloat16)
    pre = jnp.dot(agg, weight_ref[...], preferred_element_type=jnp.float32) + bias_ref[...]
    sigma = 1.0 / (1.0 + jnp.exp(-pre))
    out_ref[...] = (pre * sigma).astype(out_ref.dtype)
    grad_pre = (
        cotangent_ref[...].astype(jnp.float32) * (sigma * (1.0 + pre * (1.0 - sigma)))
    ).astype(jnp.bfloat16)
    width = grad_pre.shape[1]
    weight_grad = factor * lax.dot_general(
        agg, grad_pre, (((0,), (0,)), ((), ())), preferred_element_type=jnp.float32
    )
    grads_ref[:width] = weight_grad.astype(grads_ref.dtype)
    bias = factor * jnp.sum(grad_pre.astype(jnp.float32), axis=0, keepdims=True)
    extra = grads_ref.shape[0] - width
    first = lax.broadcasted_iota(jnp.int32, (extra, width), 0) == 0
    grads_ref[width:] = jnp.where(first, bias, 0.0).astype(grads_ref.dtype)


def layer(parts, weight, bias_term, cotangent, factor, grad_rows):
    width = weight.shape[0]
    return pl.pallas_call(
        functools.partial(layer_kernel, factor),
        out_shape=(
            jax.ShapeDtypeStruct(cotangent.shape, jnp.bfloat16),
            jax.ShapeDtypeStruct((grad_rows, width), jnp.bfloat16),
        ),
        in_specs=[VMEM] * 4,
        out_specs=(VMEM, VMEM),
        compiler_params=pltpu.CompilerParams(vmem_limit_bytes=16 * MIB),
        name="layer",
    )(parts, weight, bias_term.reshape(1, -1), cotangent)


def spread(array, axis):
    copies = jnp.broadcast_to(array[None], (lax.axis_size(axis),) + array.shape)
    return lax.all_to_all(copies, axis, split_axis=0, concat_axis=0, tiled=True)


def copies_kernel(features_ref, after_ref, out_ref):
    for n in range(out_ref.shape[0]):
        out_ref[n] = features_ref[: out_ref.shape[1]]


def spread_later(features, rows, axis, after):
    size, width = lax.axis_size(axis), features.shape[1]
    copies = pl.pallas_call(
        copies_kernel,
        out_shape=jax.ShapeDtypeStruct((size, rows, width), features.dtype),
        in_specs=[VMEM, pl.BlockSpec(memory_space=pl.ANY)],
        out_specs=VMEM,
        compiler_params=pltpu.CompilerParams(vmem_limit_bytes=8 * MIB),
        name="copies",
    )(features, after)
    return lax.all_to_all(copies, axis, split_axis=0, concat_axis=0, tiled=True)


def scattered(array, axis):
    size = lax.axis_size(axis)
    parts = array.reshape(size, array.shape[0] // size, array.shape[1])
    return lax.all_to_all(parts, axis, split_axis=0, concat_axis=0, tiled=True)


def summed(parts):
    total = parts[0].astype(jnp.float32)
    for part in parts[1:]:
        total += part.astype(jnp.float32)
    return total.astype(jnp.bfloat16)


def total_over_all(grads):
    share = summed(scattered(grads, "z"))
    share = summed(spread(share, "y"))
    share = summed(spread(share, REP))
    return spread(share, "z").reshape(grads.shape).astype(jnp.float32)


def both_ways(block, axis):
    n = lax.axis_size(axis)
    up = [(i, (i + 1) % n) for i in range(n)]
    down = [(i, (i - 1) % n) for i in range(n)]
    before, after = [block], [block]
    for _ in range(n // 2 - 1):
        before.append(lax.ppermute(before[-1], axis, up))
        after.append(lax.ppermute(after[-1], axis, down))
    half = block.shape[0] // 2
    far = [
        lax.ppermute(before[-1][:half], axis, up),
        lax.ppermute(after[-1][half:], axis, down),
    ]
    return before + after[:0:-1] + far


def shards(
    features, tile_table, weight, bias_term, cotangent, adj_rows, adj_cols, adj_tiles, adj_count
):
    own_rows, width = features.shape
    rep_size = lax.axis_size(REP)
    lists = (adj_rows, adj_tiles, adj_count)
    ny, nz = lax.axis_size("y"), lax.axis_size("z")
    kept = BLOCK + LEAD
    along_z = lax.all_gather(features[kept:], "z", axis=0, tiled=True)
    near = spread_later(features, kept, "y", along_z).reshape(ny * kept, width)
    near = lax.all_gather(near, "z", axis=0, tiled=True)
    ring = both_ways(along_z, "y")

    cols = adj_cols[0, 0]
    panel = cols // BPD
    second = cols % BPD == 1
    near_start = panel * kept + jnp.where(second, BLOCK, 0)
    behind = (lax.axis_index("y") - panel) % ny
    start = panel // ny * (own_rows - kept)
    half = ring[-1].shape[0]
    upper = start >= half
    far = behind == ny // 2
    which = jnp.where(far, ny - 1 + upper.astype(jnp.int32), behind - (behind > ny // 2))
    which = jnp.where(second, which, -1)
    start = jnp.where(far & upper, start - half, start)

    rows = rep_size * own_rows
    share = spmm(lists, near_start, which, start, near, ring, tile_table, rows)
    parts = scattered(share, REP)
    factor = 1.0 / math.sqrt(nz * ny * rows)
    grad_rows = -(-(width + 8) // (8 * nz)) * 8 * nz
    output, grads = layer(parts, weight, bias_term, cotangent, factor, grad_rows)
    grads = total_over_all(grads)
    return (output, grads[:width], grads[width])


def solution(mesh):
    panels, rep = mesh.devices.shape
    ny = 8 if panels % 8 == 0 else 2
    devices = np.asarray(mesh.devices).reshape(panels // ny, ny, rep // 2, 2)
    rows = ("z", "y")
    return jax.shard_map(
        shards,
        mesh=Mesh(devices, ("z", "y", "x", "core")),
        in_specs=(
            P(rows + REP, None),
            P(),
            P(),
            P(),
            P(rows + REP, None),
            P(rows, REP, None),
            P(rows, REP, None),
            P(rows, REP, None),
            P(rows, REP),
        ),
        out_specs=(P(rows + REP, None), P(), P()),
        check_vma=False,
    )
```

```python
import functools
import math

import jax
import jax.numpy as jnp
import numpy as np
from jax import lax
from jax.experimental import pallas as pl
from jax.experimental.pallas import tpu as pltpu
from jax.sharding import Mesh, PartitionSpec as P

BLOCK = 64
BPD = 2
UNROLL = 12
SPMM_MIB = 58
STREAMS = 2
MIB = 1024 * 1024
REP = ("x", "core")
PLANE = ("y", "x", "core")
SUB, LANES = 8, 128
SMEM = pl.BlockSpec(memory_space=pltpu.SMEM)
HBM = pl.BlockSpec(memory_space=pltpu.HBM)
VMEM = pl.BlockSpec(memory_space=pltpu.VMEM)


def choose(index, low, actions):
    if len(actions) == 1:
        actions[0]()
        return
    middle = len(actions) // 2

    @pl.when(index < low + middle)
    def _():
        choose(index, low, actions[:middle])

    @pl.when(index >= low + middle)
    def _():
        choose(index, low + middle, actions[middle:])


def spmm_kernel(
    rows_ref, tiles_ref, count_ref, which_ref, start_ref, table_ref, *refs
):
    *sources, out_ref, picked, table, total, sems, table_sem = refs
    count = count_ref[0, 0]
    steps = (count + UNROLL - 1) // UNROLL
    table_copy = pltpu.make_async_copy(table_ref, table, table_sem)
    table_copy.start()

    def fetch(s, source, start):
        return pltpu.make_async_copy(
            source.at[pl.ds(pl.multiple_of(start, BLOCK), BLOCK)], picked.at[s], sems.at[s]
        )

    def begin(s, carry):
        start = start_ref[s]
        choose(which_ref[s], 0, [fetch(s, source, start).start for source in sources])
        return carry

    lax.fori_loop(0, steps * UNROLL, begin, 0)
    total[...] = jnp.zeros_like(total)
    table_copy.wait()

    def step(i, carry):
        for k in range(UNROLL):
            fetch(i * UNROLL + k, sources[0], 0).wait()
        for k in range(UNROLL):
            s = i * UNROLL + k
            product = jnp.dot(
                table[tiles_ref[0, 0, s]], picked[s], preferred_element_type=jnp.float32
            )
            row = pl.multiple_of(rows_ref[0, 0, s] * BLOCK, BLOCK)
            total[pl.ds(row, BLOCK)] += jnp.where(s < count, product, 0.0)
        return carry

    lax.fori_loop(0, steps, step, 0)
    out_ref[...] = total[...].astype(out_ref.dtype)


def spmm(lists, which, start, sources, tile_table, out_rows):
    slots = start.shape[0]
    width = sources[0].shape[1]
    return pl.pallas_call(
        spmm_kernel,
        out_shape=jax.ShapeDtypeStruct((out_rows, width), jnp.bfloat16),
        in_specs=[SMEM] * 5 + [HBM] * (1 + len(sources)),
        out_specs=VMEM,
        scratch_shapes=[
            pltpu.VMEM((slots, BLOCK, width), jnp.bfloat16),
            pltpu.VMEM(tile_table.shape, tile_table.dtype),
            pltpu.VMEM((out_rows, width), jnp.float32),
            pltpu.SemaphoreType.DMA((slots,)),
            pltpu.SemaphoreType.DMA,
        ],
        compiler_params=pltpu.CompilerParams(vmem_limit_bytes=SPMM_MIB * MIB),
        name="spmm",
    )(*lists, which, start, tile_table, *sources)


def layer_kernel(
    factor, parts_ref, weight_ref, bias_ref, cotangent_ref, out_ref, grads_ref
):
    summed = parts_ref[0].astype(jnp.float32)
    for r in range(1, parts_ref.shape[0]):
        summed += parts_ref[r].astype(jnp.float32)
    agg = summed.astype(jnp.bfloat16)
    pre = jnp.dot(agg, weight_ref[...], preferred_element_type=jnp.float32) + bias_ref[...]
    sigma = 1.0 / (1.0 + jnp.exp(-pre))
    out_ref[...] = (pre * sigma).astype(out_ref.dtype)
    grad_pre = (
        cotangent_ref[...].astype(jnp.float32) * (sigma * (1.0 + pre * (1.0 - sigma)))
    ).astype(jnp.bfloat16)
    weight_grad = factor * lax.dot_general(
        agg, grad_pre, (((0,), (0,)), ((), ())), preferred_element_type=jnp.float32
    )
    bias = factor * jnp.sum(grad_pre.astype(jnp.float32), axis=0, keepdims=True)
    first = lax.broadcasted_iota(jnp.int32, (SUB, LANES), 0) == 0
    across = bias.shape[1] // LANES
    for n in range(grads_ref.shape[0]):
        row, col = n // across * SUB, n % across * LANES
        tile = weight_grad[row : row + SUB, col : col + LANES]
        extra = jnp.where(first, bias[:, col : col + LANES], 0.0)
        if n >= across:
            extra = jnp.zeros_like(extra)
        grads_ref[n] = jnp.concatenate([tile, extra]).astype(grads_ref.dtype)


def fold_kernel(parts_ref, out_ref):
    total = parts_ref[0].astype(jnp.float32)
    for n in range(1, parts_ref.shape[0]):
        total += parts_ref[n].astype(jnp.float32)
    for n in range(out_ref.shape[0]):
        out_ref[n] = total.astype(out_ref.dtype)


def fold(parts, copies):
    return pl.pallas_call(
        fold_kernel,
        out_shape=jax.ShapeDtypeStruct((copies,) + parts.shape[1:], parts.dtype),
        in_specs=[VMEM],
        out_specs=VMEM,
        compiler_params=pltpu.CompilerParams(vmem_limit_bytes=16 * MIB),
        name="fold",
    )(parts)


def finish_kernel(grads_ref, weight_ref, bias_ref):
    across = bias_ref.shape[1] // LANES
    for n in range(grads_ref.shape[0]):
        row, col = n // across * SUB, n % across * LANES
        tile = grads_ref[n].astype(jnp.float32)
        weight_ref[row : row + SUB, col : col + LANES] = tile[:SUB]
        if n < across:
            bias_ref[:, col : col + LANES] = tile[SUB : SUB + 1]


def finish(grads, width):
    return pl.pallas_call(
        finish_kernel,
        out_shape=(
            jax.ShapeDtypeStruct((width, width), jnp.float32),
            jax.ShapeDtypeStruct((1, width), jnp.float32),
        ),
        in_specs=[VMEM],
        out_specs=(VMEM, VMEM),
        compiler_params=pltpu.CompilerParams(vmem_limit_bytes=16 * MIB),
        name="finish",
    )(grads)


def layer(parts, weight, bias_term, cotangent, factor):
    width = weight.shape[0]
    return pl.pallas_call(
        functools.partial(layer_kernel, factor),
        out_shape=(
            jax.ShapeDtypeStruct(cotangent.shape, jnp.bfloat16),
            jax.ShapeDtypeStruct((width * width // (SUB * LANES), 2 * SUB, LANES), jnp.bfloat16),
        ),
        in_specs=[VMEM] * 4,
        out_specs=(VMEM, VMEM),
        compiler_params=pltpu.CompilerParams(vmem_limit_bytes=16 * MIB),
        name="layer",
    )(parts, weight, bias_term.reshape(1, -1), cotangent)


def scattered(array, axis):
    size = lax.axis_size(axis)
    parts = array.reshape(size, array.shape[0] // size, array.shape[1])
    return lax.all_to_all(parts, axis, split_axis=0, concat_axis=0, tiled=True)


def total_over_all(grads):
    size = lax.axis_size(PLANE)
    parts = grads.reshape(size, -1, LANES)

    def swap(array, axis):
        return lax.all_to_all(array, axis, split_axis=0, concat_axis=0, tiled=True)

    share = fold(swap(parts, PLANE), lax.axis_size("z"))
    share = fold(swap(share, "z"), size)
    return swap(share, PLANE).reshape(grads.shape)


def both_ways(block, axis, last_up):
    n = lax.axis_size(axis)
    up = [(i, (i + 1) % n) for i in range(n)]
    down = [(i, (i - 1) % n) for i in range(n)]
    before, after = [block], [block]
    for _ in range(n // 2 - 1):
        before.append(lax.ppermute(before[-1], axis, up))
        after.append(lax.ppermute(after[-1], axis, down))
    far = lax.ppermute(before[-1], axis, up) if last_up else lax.ppermute(after[-1], axis, down)
    return before + after[:0:-1] + [far]


def shards(
    features, tile_table, weight, bias_term, cotangent, adj_rows, adj_cols, adj_tiles, adj_count
):
    own_rows, width = features.shape
    rep_size = lax.axis_size(REP)
    lists = (adj_rows, adj_tiles, adj_count)
    ny, nz = lax.axis_size("y"), lax.axis_size("z")
    along_z = lax.all_gather(features, "z", axis=0, tiled=True)
    depth = along_z.shape[0] // STREAMS
    sources = []
    for n in range(STREAMS):
        sources += both_ways(along_z[n * depth : (n + 1) * depth], "y", n % 2 == 0)

    cols = adj_cols[0, 0]
    panel = cols // BPD
    start = panel // ny * own_rows + cols % BPD * BLOCK
    stream, start = start // depth, start % depth
    behind = (lax.axis_index("y") - panel) % ny
    which = jnp.where(behind == ny // 2, ny - 1, behind - (behind > ny // 2)) + stream * ny

    rows = rep_size * own_rows
    share = spmm(lists, which, start, sources, tile_table, rows)
    parts = scattered(share, REP)
    factor = 1.0 / math.sqrt(nz * ny * rows)
    output, grads = layer(parts, weight, bias_term, cotangent, factor)
    weight_grad, bias_grad = finish(total_over_all(grads), width)
    return (output, weight_grad, bias_grad.reshape(width))


def solution(mesh):
    panels, rep = mesh.devices.shape
    ny = 8 if panels % 8 == 0 else 2
    devices = np.asarray(mesh.devices).reshape(panels // ny, ny, rep // 2, 2)
    rows = ("z", "y")
    return jax.shard_map(
        shards,
        mesh=Mesh(devices, ("z", "y", "x", "core")),
        in_specs=(
            P(rows + REP, None),
            P(),
            P(),
            P(),
            P(rows + REP, None),
            P(rows, REP, None),
            P(rows, REP, None),
            P(rows, REP, None),
            P(rows, REP),
        ),
        out_specs=(P(rows + REP, None), P(), P()),
        check_vma=False,
    )
```

```python
import functools
import math

import jax
import jax.numpy as jnp
import numpy as np
from jax import lax
from jax.experimental import pallas as pl
from jax.experimental.pallas import tpu as pltpu
from jax.sharding import Mesh, PartitionSpec as P

BLOCK = 64
BPD = 2
UNROLL = 12
SPMM_MIB = 58
STREAMS = 2
MIB = 1024 * 1024
REP = ("x", "core")
PLANE = ("y", "x", "core")
SUB, LANES = 8, 128
SMEM = pl.BlockSpec(memory_space=pltpu.SMEM)
HBM = pl.BlockSpec(memory_space=pltpu.HBM)
VMEM = pl.BlockSpec(memory_space=pltpu.VMEM)


def choose(index, low, actions):
    if len(actions) == 1:
        actions[0]()
        return
    middle = len(actions) // 2

    @pl.when(index < low + middle)
    def _():
        choose(index, low, actions[:middle])

    @pl.when(index >= low + middle)
    def _():
        choose(index, low + middle, actions[middle:])


def spmm_kernel(
    rows_ref, tiles_ref, count_ref, which_ref, start_ref, table_ref, *refs
):
    *sources, out_ref, picked, table, total, sems, table_sem = refs
    count = count_ref[0, 0]
    steps = (count + UNROLL - 1) // UNROLL
    table_copy = pltpu.make_async_copy(table_ref, table, table_sem)
    table_copy.start()

    def fetch(s, source, start):
        return pltpu.make_async_copy(
            source.at[pl.ds(pl.multiple_of(start, BLOCK), BLOCK)], picked.at[s], sems.at[s]
        )

    def begin(i, carry):
        for k in range(4):
            s = i * 4 + k
            start = start_ref[s]
            choose(which_ref[s], 0, [fetch(s, source, start).start for source in sources])
        return carry

    lax.fori_loop(0, steps * (UNROLL // 4), begin, 0)
    total[...] = jnp.zeros_like(total)
    table_copy.wait()

    def step(i, carry):
        for k in range(UNROLL):
            fetch(i * UNROLL + k, sources[0], 0).wait()
        for k in range(UNROLL):
            s = i * UNROLL + k
            product = jnp.dot(
                table[tiles_ref[0, 0, s]], picked[s], preferred_element_type=jnp.float32
            )
            row = pl.multiple_of(rows_ref[0, 0, s] * BLOCK, BLOCK)
            total[pl.ds(row, BLOCK)] += jnp.where(s < count, product, 0.0)
        return carry

    lax.fori_loop(0, steps, step, 0)
    out_ref[...] = total[...].astype(out_ref.dtype)


def spmm(lists, which, start, sources, tile_table, out_rows):
    slots = start.shape[0]
    width = sources[0].shape[1]
    return pl.pallas_call(
        spmm_kernel,
        out_shape=jax.ShapeDtypeStruct((out_rows, width), jnp.bfloat16),
        in_specs=[SMEM] * 5 + [HBM] * (1 + len(sources)),
        out_specs=VMEM,
        scratch_shapes=[
            pltpu.VMEM((slots, BLOCK, width), jnp.bfloat16),
            pltpu.VMEM(tile_table.shape, tile_table.dtype),
            pltpu.VMEM((out_rows, width), jnp.float32),
            pltpu.SemaphoreType.DMA((slots,)),
            pltpu.SemaphoreType.DMA,
        ],
        compiler_params=pltpu.CompilerParams(vmem_limit_bytes=SPMM_MIB * MIB),
        name="spmm",
    )(*lists, which, start, tile_table, *sources)


def layer_kernel(
    factor, parts_ref, weight_ref, bias_ref, cotangent_ref, out_ref, grads_ref
):
    summed = parts_ref[0].astype(jnp.float32)
    for r in range(1, parts_ref.shape[0]):
        summed += parts_ref[r].astype(jnp.float32)
    agg = summed.astype(jnp.bfloat16)
    pre = jnp.dot(agg, weight_ref[...], preferred_element_type=jnp.float32) + bias_ref[...]
    sigma = 1.0 / (1.0 + jnp.exp(-pre))
    out_ref[...] = (pre * sigma).astype(out_ref.dtype)
    grad_pre = (
        cotangent_ref[...].astype(jnp.float32) * (sigma * (1.0 + pre * (1.0 - sigma)))
    ).astype(jnp.bfloat16)
    weight_grad = factor * lax.dot_general(
        agg, grad_pre, (((0,), (0,)), ((), ())), preferred_element_type=jnp.float32
    )
    bias = factor * jnp.sum(grad_pre.astype(jnp.float32), axis=0, keepdims=True)
    first = lax.broadcasted_iota(jnp.int32, (SUB, LANES), 0) == 0
    across = bias.shape[1] // LANES
    for n in range(grads_ref.shape[0]):
        row, col = n // across * SUB, n % across * LANES
        tile = weight_grad[row : row + SUB, col : col + LANES]
        extra = jnp.where(first, bias[:, col : col + LANES], 0.0)
        if n >= across:
            extra = jnp.zeros_like(extra)
        grads_ref[n] = jnp.concatenate([tile, extra]).astype(grads_ref.dtype)


def fold_kernel(parts_ref, out_ref):
    total = parts_ref[0].astype(jnp.float32)
    for n in range(1, parts_ref.shape[0]):
        total += parts_ref[n].astype(jnp.float32)
    for n in range(out_ref.shape[0]):
        out_ref[n] = total.astype(out_ref.dtype)


def fold(parts, copies):
    return pl.pallas_call(
        fold_kernel,
        out_shape=jax.ShapeDtypeStruct((copies,) + parts.shape[1:], parts.dtype),
        in_specs=[VMEM],
        out_specs=VMEM,
        compiler_params=pltpu.CompilerParams(vmem_limit_bytes=16 * MIB),
        name="fold",
    )(parts)


def finish_kernel(grads_ref, weight_ref, bias_ref):
    across = bias_ref.shape[1] // LANES
    for n in range(grads_ref.shape[0]):
        row, col = n // across * SUB, n % across * LANES
        tile = grads_ref[n].astype(jnp.float32)
        weight_ref[row : row + SUB, col : col + LANES] = tile[:SUB]
        if n < across:
            bias_ref[:, col : col + LANES] = tile[SUB : SUB + 1]


def finish(grads, width):
    return pl.pallas_call(
        finish_kernel,
        out_shape=(
            jax.ShapeDtypeStruct((width, width), jnp.float32),
            jax.ShapeDtypeStruct((1, width), jnp.float32),
        ),
        in_specs=[VMEM],
        out_specs=(VMEM, VMEM),
        compiler_params=pltpu.CompilerParams(vmem_limit_bytes=16 * MIB),
        name="finish",
    )(grads)


def layer(parts, weight, bias_term, cotangent, factor):
    width = weight.shape[0]
    return pl.pallas_call(
        functools.partial(layer_kernel, factor),
        out_shape=(
            jax.ShapeDtypeStruct(cotangent.shape, jnp.bfloat16),
            jax.ShapeDtypeStruct((width * width // (SUB * LANES), 2 * SUB, LANES), jnp.bfloat16),
        ),
        in_specs=[VMEM] * 4,
        out_specs=(VMEM, VMEM),
        compiler_params=pltpu.CompilerParams(vmem_limit_bytes=16 * MIB),
        name="layer",
    )(parts, weight, bias_term.reshape(1, -1), cotangent)


def scattered(array, axis):
    size = lax.axis_size(axis)
    parts = array.reshape(size, array.shape[0] // size, array.shape[1])
    return lax.all_to_all(parts, axis, split_axis=0, concat_axis=0, tiled=True)


def total_over_all(grads):
    size = lax.axis_size(PLANE)
    parts = grads.reshape(size, -1, LANES)

    def swap(array, axis):
        return lax.all_to_all(array, axis, split_axis=0, concat_axis=0, tiled=True)

    share = fold(swap(parts, PLANE), lax.axis_size("z"))
    share = fold(swap(share, "z"), size)
    return swap(share, PLANE).reshape(grads.shape)


def both_ways(block, axis, last_up):
    n = lax.axis_size(axis)
    up = [(i, (i + 1) % n) for i in range(n)]
    down = [(i, (i - 1) % n) for i in range(n)]
    before, after = [block], [block]
    for _ in range(n // 2 - 1):
        before.append(lax.ppermute(before[-1], axis, up))
        after.append(lax.ppermute(after[-1], axis, down))
    far = lax.ppermute(before[-1], axis, up) if last_up else lax.ppermute(after[-1], axis, down)
    return before + after[:0:-1] + [far]


def shards(
    features, tile_table, weight, bias_term, cotangent, adj_rows, adj_cols, adj_tiles, adj_count
):
    own_rows, width = features.shape
    rep_size = lax.axis_size(REP)
    lists = (adj_rows, adj_tiles, adj_count)
    ny, nz = lax.axis_size("y"), lax.axis_size("z")
    along_z = lax.all_gather(features, "z", axis=0, tiled=True)
    depth = along_z.shape[0] // STREAMS
    sources = []
    for n in range(STREAMS):
        sources += both_ways(along_z[n * depth : (n + 1) * depth], "y", n % 2 == 0)

    cols = adj_cols[0, 0]
    panel = cols // BPD
    start = panel // ny * own_rows + cols % BPD * BLOCK
    stream, start = start // depth, start % depth
    behind = (lax.axis_index("y") - panel) % ny
    which = jnp.where(behind == ny // 2, ny - 1, behind - (behind > ny // 2)) + stream * ny

    rows = rep_size * own_rows
    share = spmm(lists, which, start, sources, tile_table, rows)
    parts = scattered(share, REP)
    factor = 1.0 / math.sqrt(nz * ny * rows)
    output, grads = layer(parts, weight, bias_term, cotangent, factor)
    weight_grad, bias_grad = finish(total_over_all(grads), width)
    return (output, weight_grad, bias_grad.reshape(width))


def solution(mesh):
    panels, rep = mesh.devices.shape
    ny = 8 if panels % 8 == 0 else 2
    devices = np.asarray(mesh.devices).reshape(panels // ny, ny, rep // 2, 2)
    rows = ("z", "y")
    return jax.shard_map(
        shards,
        mesh=Mesh(devices, ("z", "y", "x", "core")),
        in_specs=(
            P(rows + REP, None),
            P(),
            P(),
            P(),
            P(rows + REP, None),
            P(rows, REP, None),
            P(rows, REP, None),
            P(rows, REP, None),
            P(rows, REP),
        ),
        out_specs=(P(rows + REP, None), P(), P()),
        check_vma=False,
    )
```
